32 devices in a mesh: tile: 8 (over z, y), segment: 4 (over x, core).
Axes of the slice: x: 2, y: 2, z: 4, core: 2. Of those that a mesh axis runs over, the one named last changes fastest.
Arguments:
- cube: float32 [16, 96, 1024], P(None, 'tile'), may hold values from -6 to 6
- footprint: int32 [16, 1024], replicated, may hold values 0 or 1
- lift_weight: float32 [32], replicated, may hold values from -4 to 4
- lift_bias: float32 [32], replicated, may hold values from -2 to 2
- spatial_weight: bfloat16 [8, 32, 288], P('segment'), may hold values from -0.375 to 0.375
- spatial_bias: bfloat16 [8, 32], P('segment'), may hold values from -2 to 2
- spectral_weight: bfloat16 [8, 32, 96], P('segment'), may hold values from -1.5 to 1.5
- head_weight: float32 [32], replicated, may hold values from -1 to 1
Outputs:
- scores: float32 [16, 96, 1024], P('segment', 'tile')
The draws below stay inside these ranges and needn't reach their ends.
All inputs are finite; a program needn't handle non-finite values.
Results may differ from the reference program's by a relative error of at most 0.035.
Values may be sent and summed in bfloat16 or wider, within the bound.
A program may use at most 64 MiB of HBM per device.

```python
import jax
import jax.numpy as jnp
from jax import lax

C = 32
SKY = 32
MICRO = 16
LAYERS = 8
NFREQ = 96
P_SIZE = 1024


def touch_ends(entries, key, low, largest):
    spot = [jax.random.randint(jax.random.fold_in(key, axis), (), 0, length) for axis, length in enumerate(entries.shape)]
    longest = entries.shape.index(max(entries.shape))
    beside = spot[:longest] + [(spot[longest] + 1) % entries.shape[longest]] + spot[longest + 1:]
    return entries.at[tuple(spot)].set(low).at[tuple(beside)].set(largest)


def shard_levels(key, shape, pieces, least, high):
    gain, own = 1.0, jax.random.fold_in(key, 6)
    for axis_at, parts in pieces:
        draws = jnp.exp(jax.random.uniform(jax.random.fold_in(own, axis_at), (parts,), jnp.float32, least / len(pieces), high / len(pieces)))
        gain = gain * jnp.repeat(draws, shape[axis_at] // parts).reshape([-1 if axis == axis_at else 1 for axis in range(len(shape))])
    return gain


def normal_values(stream_key, dims, deviation, most, split=(), dtype=jnp.bfloat16):
    array = deviation * jax.random.normal(stream_key, dims, jnp.float32)
    if split:
        array = array * shard_levels(stream_key, dims, split, -0.22, 0.18)
    return jnp.clip(array, -most, most).astype(dtype)


def setup_inputs(seed: int = 0) -> dict:
    key_of = jax.random.split(jax.random.key(seed), 9)
    return {
        "cube": normal_values(key_of[0], (MICRO, NFREQ, P_SIZE), 1.0, 6.0, ((1, 8),), jnp.float32),
        "footprint": touch_ends((jax.random.randint(key_of[1], (MICRO, P_SIZE), 0, 4) < 3).astype(jnp.int32), jax.random.fold_in(key_of[1], 1), 0, 1),
        "lift_weight": normal_values(key_of[2], (C,), 1.0, 4.0, (), jnp.float32),
        "lift_bias": normal_values(key_of[3], (C,), 0.25, 2.0, (), jnp.float32),
        "spatial_weight": normal_values(key_of[4], (LAYERS, C, 9 * C), (9 * C) ** -0.5, 0.375, ((0, 4),)),
        "spatial_bias": normal_values(key_of[5], (LAYERS, C), 0.25, 2.0, ((0, 4),)),
        "spectral_weight": normal_values(key_of[6], (LAYERS, C, 3 * C), ((1.6 / (3 * C)) ** 0.5), 1.5, ((0, 4),)),
        "head_weight": normal_values(key_of[7], (C,), C ** -0.5, 1.0, (), jnp.float32),
    }


def spatial_conv(field, weight, bias_row):
    planes = field.shape[0]
    images = field.reshape(planes, C, SKY, SKY)
    kernel = weight.astype(jnp.float32).reshape(C, 3, 3, C).transpose(0, 3, 1, 2)
    summed = lax.conv_general_dilated(images, kernel, (1, 1), ((1, 1), (1, 1)), dimension_numbers=("NCHW", "OIHW", "NCHW"), precision=lax.Precision.HIGHEST)
    return summed.reshape(planes, C, SKY * SKY) + bias_row.astype(jnp.float32)[None, :, None]


def reference(cube, footprint, lift_weight, lift_bias, spatial_weight, spatial_bias, spectral_weight, head_weight):
    def per_field(inputs):
        plane, flags = inputs
        keep_mask = flags.astype(jnp.float32)[None, None, :]
        field = (keep_mask * (lift_weight[None, :, None] * plane[:, None, :] + lift_bias[None, :, None])).astype(jnp.bfloat16)
        for layer in range(LAYERS):
            wide = lax.optimization_barrier(field).astype(jnp.float32)
            summed = spatial_conv(wide, spatial_weight[layer], spatial_bias[layer])
            gated = lax.optimization_barrier(jax.nn.silu(summed).astype(jnp.bfloat16)).astype(jnp.float32)
            padded = jnp.pad(gated, ((1, 1), (0, 0), (0, 0)))
            spec_weight = spectral_weight[layer].astype(jnp.float32)
            mixed = jnp.zeros_like(wide)
            for side in range(3):
                mixed = mixed + jnp.einsum("oi,nip->nop", spec_weight[:, side * C:(side + 1) * C], padded[side:side + NFREQ], precision=lax.Precision.HIGHEST)
            field = (keep_mask * (0.5 * wide + mixed)).astype(jnp.bfloat16)
        return jnp.einsum("c,ncp->np", head_weight, field.astype(jnp.float32), precision=lax.Precision.HIGHEST)

    return lax.map(per_field, (cube, footprint))
```

```python
import functools

import jax
import jax.numpy as jnp
from jax import lax
from jax.experimental import pallas as pl
from jax.experimental.pallas import tpu as pltpu
from jax.sharding import PartitionSpec as P

SKY = 32
CH = 32
F32 = jnp.float32
BF16 = jnp.bfloat16
HALF0 = [(0, y) for y in (0, 1, 2, 3)]
HALF1 = [(1, y) for y in (2, 3, 0, 1)]
OUT_POS = HALF0 + HALF1
IN_POS = (
    OUT_POS
    + [(-1, y) for y in (2, 3, 0, 1)]
    + [(2, y) for y in (0, 1, 2, 3)]
    + [(0, 4), (1, -1), (1, 4), (0, -1)]
    + [(2, 4), (-1, -1), (-1, 4), (2, -1)]
)


def dot(a, b, dims=((1,), (0,))):
    return lax.dot_general(a, b, (dims, ((), ())), preferred_element_type=F32)


def lane_block(shape):
    return lax.broadcasted_iota(jnp.int32, shape, len(shape) - 1) // CH


def split2(x):
    hi = x.astype(BF16)
    return hi, (x - hi.astype(F32)).astype(BF16)


def shift_rows(x, amount, group):
    row = lax.broadcasted_iota(jnp.int32, x.shape, 1)
    moved = pltpu.roll(x.astype(F32), amount % 16, axis=1)
    at = (row % group) - amount
    return jnp.where((at >= 0) & (at < group), moved, 0.0).astype(BF16)


def windows(hb):
    n = hb.shape[0]
    hb = hb.reshape(n, 2, 4, 16, 256)
    half0, half1 = hb[..., :128], hb[..., 128:]
    blk = lane_block((16, 128))[None, None, None]
    outer = jnp.broadcast_to((blk == 0) | (blk == 3), half0.shape)
    edge = jnp.where(outer, half0, half1)

    def shifted(part, amount, group):
        lead = part.shape[:-2]
        flat = part.reshape((-1, 16, 128))
        return shift_rows(flat, amount, group).reshape(lead + (16, 128))

    above = jnp.concatenate([shifted(edge[:, 1:2], 4, 16), edge[:, 0:1]], axis=1)
    below = jnp.concatenate([edge[:, 1:2], shifted(edge[:, 0:1], -4, 16)], axis=1)
    top = jnp.broadcast_to((blk == 1) | (blk == 3), half0.shape)
    rim = jnp.where(top, above, below)

    def from_left(part):
        return jnp.concatenate([shifted(part[:, :, 3:4], 1, 4), part[:, :, 0:3]], axis=2)

    def from_right(part):
        return jnp.concatenate([part[:, :, 1:4], shifted(part[:, :, 0:1], -1, 4)], axis=2)

    corner = jnp.where(outer, from_right(rim), from_left(rim))
    pieces = [half0, half1, from_left(half1), from_right(half0), rim, corner]
    return jnp.concatenate([p.reshape(n * 128, 128) for p in pieces], axis=1)


def network(
    own,
    reach,
    origin_ref,
    x_ref,
    keep_ref,
    lanes_ref,
    sw_ref,
    sb_ref,
    cw_ref,
    out_ref,
    h_ref,
    g_ref,
    w1_ref,
    w2_ref,
    k_ref,
    xs_ref,
    os_ref,
    perm_ref,
):
    wide = x_ref.shape[0]
    layers = sw_ref.shape[0]
    sides = (wide - own) // reach if reach else 0
    offset = origin_ref[0]

    p = lax.broadcasted_iota(jnp.int32, (1024, 1024), 0)
    y, x = p // SKY, p % SKY
    x2 = x % 2
    nb = x2 * 4 + ((y % 4) + 2 * x2) % 4
    r = (((y // 4) % 2) * 4 + (x // 2) % 4) * 16 + (y // 8) * 4 + x // 8
    q = lax.broadcasted_iota(jnp.int32, (1024, 1024), 1)
    perm_ref[...] = jnp.where(nb * 128 + r == q, 1.0, 0.0).astype(BF16)

    hi, lo = split2(x_ref[...])
    xp = dot(hi, perm_ref[...]) + dot(lo, perm_ref[...])
    for j in range(8):
        xs_ref[:, j, :] = xp[:, j * 128 : (j + 1) * 128]
    kp = dot(jnp.broadcast_to(keep_ref[...], (16, 1024)).astype(BF16), perm_ref[...])
    expand = jnp.where(
        lane_block((8, 256)) == lax.broadcasted_iota(jnp.int32, (8, 256), 0), 1.0, 0.0
    ).astype(BF16)
    k8 = jnp.concatenate([kp[0:1, j * 128 : (j + 1) * 128] for j in range(8)], axis=0)
    k_ref[...] = dot(k8.T.astype(BF16), expand).astype(BF16).reshape(8, 16, 256)

    lift_w, lift_b = lanes_ref[0:1, :], lanes_ref[1:2, :]

    def lift(f, _):
        hi, lo = split2(xs_ref[f].T)
        full = dot(hi, expand) + dot(lo, expand)
        fresh = (lift_w * full + lift_b).astype(BF16).reshape(8, 16, 256)
        h_ref[f] = fresh * k_ref[...]
        return 0

    lax.fori_loop(0, wide, lift, 0, unroll=4)
    g_ref[0] = jnp.zeros(g_ref.shape[1:], BF16)
    g_ref[wide + 1] = jnp.zeros(g_ref.shape[1:], BF16)

    spread = jnp.where(
        lax.broadcasted_iota(jnp.int32, (CH, 256), 1) % CH
        == lax.broadcasted_iota(jnp.int32, (CH, 256), 0),
        1.0,
        0.0,
    ).astype(BF16)
    block = lane_block((CH, 256))

    def layer_step(layer, _):
        taps = 0.5 * dot(sw_ref[layer].astype(F32).T.astype(BF16), spread)
        for kb, (xi, yi) in enumerate(IN_POS):
            rows = jnp.zeros((CH, 256), F32)
            for nb, (xo, yo) in enumerate(OUT_POS):
                a, b = yi - yo, xi - xo
                if abs(a) <= 1 and abs(b) <= 1:
                    tap = (a + 1) * 3 + b + 1
                    rows = jnp.where(block == nb, taps[tap * CH : (tap + 1) * CH], rows)
            w1_ref[kb * CH : (kb + 1) * CH, :] = rows.astype(BF16)
        taps = dot(cw_ref[layer].astype(F32).T.astype(BF16), spread)
        for kf in range(4):
            for kpos in range(4):
                rows = jnp.zeros((CH, 256), F32)
                for nf in range(2):
                    tap = kf - nf
                    if 0 <= tap <= 2:
                        rows = jnp.where(
                            block == nf * 4 + kpos, taps[tap * CH : (tap + 1) * CH], rows
                        )
                kb = kf * 4 + kpos
                w2_ref[kb * CH : (kb + 1) * CH, :] = rows.astype(BF16)
        bias = 0.5 * dot(sb_ref[layer], spread)[0:1]

        left = reach - layer if reach else 0
        count = own + sides * left
        count = count + count % 2
        start = jnp.minimum(jnp.maximum(offset - left, 0), wide - count)
        pairs = count // 2

        def gate(f):
            t = dot(windows(h_ref[pl.ds(f, 2)]), w1_ref[...]) + bias
            return (t + t * jnp.tanh(t)).astype(BF16).reshape(2, 8, 16, 256)

        def mix(f):
            gb = g_ref[pl.ds(f, 4)]
            halves = [
                jnp.concatenate(
                    [gb[k, :, :, s * 128 : (s + 1) * 128].reshape(128, 128) for k in range(4)],
                    axis=1,
                )
                for s in range(2)
            ]
            v = dot(jnp.concatenate(halves, axis=0), w2_ref[...])
            planes = [
                jnp.concatenate(
                    [v[s * 128 : (s + 1) * 128, n * 128 : (n + 1) * 128] for s in range(2)], axis=1
                )
                for n in range(2)
            ]
            v = jnp.stack(planes).reshape(2, 8, 16, 256)
            old = h_ref[pl.ds(f, 2)].astype(F32)
            return (0.5 * old + v).astype(BF16) * k_ref[...][None]

        def put_gate(i):
            f = start + 2 * i
            g_ref[pl.ds(f + 1, 2)] = gate(f)

        def put_mix(i):
            f = start + 2 * i
            h_ref[pl.ds(f, 2)] = mix(f)

        def both(i, _):
            f, f2 = start + 2 * i, start + 2 * i - 4
            new_h = mix(f2)
            new_g = gate(f)
            h_ref[pl.ds(f2, 2)] = new_h
            g_ref[pl.ds(f + 1, 2)] = new_g
            return 0

        put_gate(0)
        put_gate(1)
        lax.fori_loop(2, pairs, both, 0)
        put_mix(pairs - 2)
        put_mix(pairs - 1)
        return 0

    lax.fori_loop(0, layers, layer_step, 0)

    head = jnp.where(
        lane_block((8, 256)) == lax.broadcasted_iota(jnp.int32, (8, 256), 0), lanes_ref[2:3, :], 0.0
    )
    head_hi, head_lo = split2(head)
    heads = jnp.concatenate([head_hi.astype(F32), head_lo.astype(F32)], axis=0).astype(BF16)

    def score(f, _):
        both_parts = dot(heads, h_ref[offset + f].reshape(128, 256), ((1,), (1,)))
        os_ref[f] = both_parts[0:8] + both_parts[8:16]
        return 0

    lax.fori_loop(0, own, score, 0, unroll=4)
    tiled = jnp.concatenate([os_ref[:, j, :] for j in range(8)], axis=1)
    hi, lo = split2(tiled)
    back = ((1,), (1,))
    out_ref[...] = dot(hi, perm_ref[...], back) + dot(lo, perm_ref[...], back)


def run_network(own, reach, origin, x, keep, lanes, sw, sb, cw):
    wide = x.shape[0]
    vmem = pl.BlockSpec(memory_space=pltpu.VMEM)
    return pl.pallas_call(
        functools.partial(network, own, reach),
        out_shape=jax.ShapeDtypeStruct((own, 1024), F32),
        in_specs=[pl.BlockSpec(memory_space=pltpu.SMEM)] + [vmem] * 6,
        out_specs=vmem,
        scratch_shapes=[
            pltpu.VMEM((wide, 8, 16, 256), BF16),
            pltpu.VMEM((wide + 2, 8, 16, 256), BF16),
            pltpu.VMEM((768, 256), BF16),
            pltpu.VMEM((512, 256), BF16),
            pltpu.VMEM((8, 16, 256), BF16),
            pltpu.VMEM((wide, 8, 128), F32),
            pltpu.VMEM((own, 8, 128), F32),
            pltpu.VMEM((1024, 1024), BF16),
        ],
        compiler_params=pltpu.CompilerParams(vmem_limit_bytes=48 * 1024 * 1024),
    )(origin, x, keep, lanes, sw, sb, cw)


def per_device(
    cube,
    footprint,
    lift_weight,
    lift_bias,
    spatial_weight,
    spatial_bias,
    spectral_weight,
    head_weight,
):
    micro, planes, pixels = cube.shape
    segments = lax.axis_size("segment")
    tiles = lax.axis_size("tile")
    segment = lax.axis_index("segment")
    tile = lax.axis_index("tile")
    fields = micro // segments
    groups = tiles // fields
    own = planes * fields

    sw = lax.all_gather(spatial_weight, "segment", axis=0, tiled=True)
    sb = lax.all_gather(spatial_bias, "segment", axis=0, tiled=True)
    cw = lax.all_gather(spectral_weight, "segment", axis=0, tiled=True)
    layers = sw.shape[0]

    reach = layers if groups > 1 else 0
    wide = own + reach * min(2, groups - 1)
    mine = lax.dynamic_slice_in_dim(cube, segment * fields, fields, 0)
    whole = lax.all_to_all(
        jnp.concatenate([mine] * groups, axis=0), "tile", 0, 0, tiled=True
    ).reshape(tiles * planes, pixels)
    first = (tile // fields) * own
    begin = jnp.clip(first - reach, 0, tiles * planes - wide)
    x = lax.dynamic_slice_in_dim(whole, begin, wide, 0)
    keep = lax.dynamic_slice_in_dim(footprint, segment * fields + tile % fields, 1, 0).astype(F32)
    lanes = jnp.tile(jnp.stack([lift_weight, lift_bias, head_weight]), (1, 8))
    bias = jnp.broadcast_to(sb[:, None, :], (layers, 16, CH))
    out = run_network(
        own, reach, (first - begin).astype(jnp.int32)[None], x, keep, lanes, sw, bias, cw
    )
    cliques = [[g * fields + i for i in range(fields)] for g in range(groups)]
    return lax.all_to_all(
        out.reshape(fields, planes, pixels), "tile", 0, 0, axis_index_groups=cliques, tiled=True
    )


def solution(mesh):
    placed = (
        P(None, "tile", None),
        P(),
        P(),
        P(),
        P("segment", None, None),
        P("segment", None),
        P("segment", None, None),
        P(),
    )
    return jax.shard_map(
        per_device,
        mesh=mesh,
        in_specs=placed,
        out_specs=P("segment", "tile", None),
        check_vma=False,
    )
```

```python
import functools

import jax
import jax.numpy as jnp
from jax import lax
from jax.experimental import pallas as pl
from jax.experimental.pallas import tpu as pltpu
from jax.sharding import PartitionSpec as P

SKY = 32
STEP = 4
CH = 32
F32 = jnp.float32
BF16 = jnp.bfloat16
HALF0 = [(0, y) for y in (0, 1, 2, 3)]
HALF1 = [(1, y) for y in (2, 3, 0, 1)]
OUT_POS = HALF0 + HALF1
IN_POS = (
    OUT_POS
    + [(-1, y) for y in (2, 3, 0, 1)]
    + [(2, y) for y in (0, 1, 2, 3)]
    + [(0, 4), (1, -1), (1, 4), (0, -1)]
    + [(2, 4), (-1, -1), (-1, 4), (2, -1)]
)


def dot(a, b, dims=((1,), (0,))):
    return lax.dot_general(a, b, (dims, ((), ())), preferred_element_type=F32)


def lane_block(shape):
    return lax.broadcasted_iota(jnp.int32, shape, len(shape) - 1) // CH


def split2(x):
    hi = x.astype(BF16)
    return hi, (x - hi.astype(F32)).astype(BF16)


def shift_rows(x, amount, group):
    row = lax.broadcasted_iota(jnp.int32, x.shape, 1)
    moved = pltpu.roll(x.astype(F32), amount % 16, axis=1)
    at = (row % group) - amount
    return jnp.where((at >= 0) & (at < group), moved, 0.0).astype(BF16)


def windows(hb):
    n = hb.shape[0]
    hb = hb.reshape(n, 2, 4, 16, 256)
    half0, half1 = hb[..., :128], hb[..., 128:]
    blk = lane_block((16, 128))[None, None, None]
    outer = jnp.broadcast_to((blk == 0) | (blk == 3), half0.shape)
    edge = jnp.where(outer, half0, half1)

    def shifted(part, amount, group):
        lead = part.shape[:-2]
        flat = part.reshape((-1, 16, 128))
        return shift_rows(flat, amount, group).reshape(lead + (16, 128))

    above = jnp.concatenate([shifted(edge[:, 1:2], 4, 16), edge[:, 0:1]], axis=1)
    below = jnp.concatenate([edge[:, 1:2], shifted(edge[:, 0:1], -4, 16)], axis=1)
    top = jnp.broadcast_to((blk == 1) | (blk == 3), half0.shape)
    rim = jnp.where(top, above, below)

    def from_left(part):
        return jnp.concatenate([shifted(part[:, :, 3:4], 1, 4), part[:, :, 0:3]], axis=2)

    def from_right(part):
        return jnp.concatenate([part[:, :, 1:4], shifted(part[:, :, 0:1], -1, 4)], axis=2)

    corner = jnp.where(outer, from_right(rim), from_left(rim))
    pieces = [half0, half1, from_left(half1), from_right(half0), rim, corner]
    return jnp.concatenate([p.reshape(n * 128, 128) for p in pieces], axis=1)


def network(
    own,
    reach,
    wide,
    origin_ref,
    x_ref,
    footprint_ref,
    lanes_ref,
    sw_ref,
    sb_ref,
    cw_ref,
    out_ref,
    h_ref,
    g_ref,
    w1_ref,
    w2_ref,
    k_ref,
    xs_ref,
    os_ref,
    perm_ref,
):
    layers = sw_ref.shape[0]
    depth = sb_ref.shape[1]
    sides = (wide - own) // reach if reach else 0
    offset, skip, member = origin_ref[0], origin_ref[1], origin_ref[2]

    p = lax.broadcasted_iota(jnp.int32, (1024, 1024), 0)
    y, x = p // SKY, p % SKY
    x2 = x % 2
    nb = x2 * 4 + ((y % 4) + 2 * x2) % 4
    r = (((y // 4) % 2) * 4 + (x // 2) % 4) * 16 + (y // 8) * 4 + x // 8
    q = lax.broadcasted_iota(jnp.int32, (1024, 1024), 1)
    perm_ref[...] = jnp.where(nb * 128 + r == q, 1.0, 0.0).astype(BF16)

    hi, lo = split2(jnp.concatenate([x_ref[s] for s in range(x_ref.shape[0])], axis=0))
    xp = dot(hi, perm_ref[...]) + dot(lo, perm_ref[...])
    for j in range(8):
        xs_ref[:, j, :] = xp[:, j * 128 : (j + 1) * 128]
    keep = footprint_ref[pl.ds(member, 1), :].astype(F32)
    kp = dot(jnp.broadcast_to(keep, (16, 1024)).astype(BF16), perm_ref[...])
    expand = jnp.where(
        lane_block((8, 256)) == lax.broadcasted_iota(jnp.int32, (8, 256), 0), 1.0, 0.0
    ).astype(BF16)
    k8 = jnp.concatenate([kp[0:1, j * 128 : (j + 1) * 128] for j in range(8)], axis=0)
    k_ref[...] = dot(k8.T.astype(BF16), expand).astype(BF16).reshape(8, 16, 256)

    lift_w, lift_b = lanes_ref[0:1, :], lanes_ref[1:2, :]

    def lift(f, _):
        hi, lo = split2(xs_ref[skip + f].T)
        full = dot(hi, expand) + dot(lo, expand)
        fresh = (lift_w * full + lift_b).astype(BF16).reshape(8, 16, 256)
        h_ref[f] = fresh * k_ref[...]
        return 0

    lax.fori_loop(0, wide, lift, 0, unroll=4)
    g_ref[0] = jnp.zeros(g_ref.shape[1:], BF16)
    g_ref[wide + 1] = jnp.zeros(g_ref.shape[1:], BF16)

    spread = jnp.where(
        lax.broadcasted_iota(jnp.int32, (CH, 256), 1) % CH
        == lax.broadcasted_iota(jnp.int32, (CH, 256), 0),
        1.0,
        0.0,
    ).astype(BF16)
    block = lane_block((CH, 256))

    def layer_step(layer, _):
        taps = 0.5 * dot(sw_ref[layer].astype(F32).T.astype(BF16), spread)
        for kb, (xi, yi) in enumerate(IN_POS):
            rows = jnp.zeros((CH, 256), F32)
            for nb, (xo, yo) in enumerate(OUT_POS):
                a, b = yi - yo, xi - xo
                if abs(a) <= 1 and abs(b) <= 1:
                    tap = (a + 1) * 3 + b + 1
                    rows = jnp.where(block == nb, taps[tap * CH : (tap + 1) * CH], rows)
            w1_ref[kb * CH : (kb + 1) * CH, :] = rows.astype(BF16)
        taps = dot(cw_ref[layer].astype(F32).T.astype(BF16), spread)
        for kf in range(4):
            for kpos in range(4):
                rows = jnp.zeros((CH, 256), F32)
                for nf in range(2):
                    tap = kf - nf
                    if 0 <= tap <= 2:
                        rows = jnp.where(
                            block == nf * 4 + kpos, taps[tap * CH : (tap + 1) * CH], rows
                        )
                kb = kf * 4 + kpos
                w2_ref[kb * CH : (kb + 1) * CH, :] = rows.astype(BF16)
        rows = sb_ref[layer // depth].astype(F32)
        here = lax.broadcasted_iota(jnp.int32, rows.shape, 0) == layer % depth
        row = jnp.sum(jnp.where(here, rows, 0.0), axis=0, keepdims=True)
        bias = 0.5 * dot(jnp.broadcast_to(row, (16, CH)).astype(BF16), spread)[0:1]

        left = reach - layer if reach else 0
        count = own + sides * left
        count = (count + STEP - 1) // STEP * STEP
        start = jnp.minimum(jnp.maximum(offset - left, 0), wide - count)
        steps = count // STEP

        def gate(f):
            t = dot(windows(h_ref[pl.ds(f, STEP)]), w1_ref[...]) + bias
            return (t + t * jnp.tanh(t)).astype(BF16).reshape(STEP, 8, 16, 256)

        def mix(f):
            gb = g_ref[pl.ds(f, STEP + 2)]
            halves = [
                jnp.concatenate(
                    [
                        gb[n + k, :, :, s * 128 : (s + 1) * 128].reshape(128, 128)
                        for k in range(4)
                    ],
                    axis=1,
                )
                for n in range(0, STEP, 2)
                for s in range(2)
            ]
            v = dot(jnp.concatenate(halves, axis=0), w2_ref[...])
            planes = [
                jnp.concatenate(
                    [
                        v[(n + s) * 128 : (n + s + 1) * 128, m * 128 : (m + 1) * 128]
                        for s in range(2)
                    ],
                    axis=1,
                )
                for n in range(0, STEP, 2)
                for m in range(2)
            ]
            v = jnp.stack(planes).reshape(STEP, 8, 16, 256)
            old = h_ref[pl.ds(f, STEP)].astype(F32)
            return (0.5 * old + v).astype(BF16) * k_ref[...][None]

        def put_gate(i):
            f = start + STEP * i
            g_ref[pl.ds(f + 1, STEP)] = gate(f)

        def put_mix(i):
            f = start + STEP * i
            h_ref[pl.ds(f, STEP)] = mix(f)

        def both(i, _):
            f, f2 = start + STEP * i, start + STEP * (i - 2)
            new_h = mix(f2)
            new_g = gate(f)
            h_ref[pl.ds(f2, STEP)] = new_h
            g_ref[pl.ds(f + 1, STEP)] = new_g
            return 0

        put_gate(0)
        put_gate(1)
        lax.fori_loop(2, steps, both, 0)
        put_mix(steps - 2)
        put_mix(steps - 1)
        return 0

    lax.fori_loop(0, layers, layer_step, 0)

    head = jnp.where(
        lane_block((8, 256)) == lax.broadcasted_iota(jnp.int32, (8, 256), 0), lanes_ref[2:3, :], 0.0
    )
    head_hi, head_lo = split2(head)
    heads = jnp.concatenate([head_hi.astype(F32), head_lo.astype(F32)], axis=0).astype(BF16)

    def score(f, _):
        both_parts = dot(heads, h_ref[offset + f].reshape(128, 256), ((1,), (1,)))
        os_ref[f] = both_parts[0:8] + both_parts[8:16]
        return 0

    lax.fori_loop(0, own, score, 0, unroll=4)
    tiled = jnp.concatenate([os_ref[:, j, :] for j in range(8)], axis=1)
    hi, lo = split2(tiled)
    back = ((1,), (1,))
    scores = dot(hi, perm_ref[...], back) + dot(lo, perm_ref[...], back)
    planes = out_ref.shape[1]
    for s in range(out_ref.shape[0]):
        out_ref[s] = scores[s * planes : (s + 1) * planes]


def run_network(own, reach, wide, origin, x, footprint, lanes, sw, sb, cw):
    slots, planes = x.shape[:2]
    vmem = pl.BlockSpec(memory_space=pltpu.VMEM)
    return pl.pallas_call(
        functools.partial(network, own, reach, wide),
        out_shape=jax.ShapeDtypeStruct((own // planes, planes, 1024), F32),
        in_specs=[pl.BlockSpec(memory_space=pltpu.SMEM)] + [vmem] * 6,
        out_specs=vmem,
        scratch_shapes=[
            pltpu.VMEM((wide, 8, 16, 256), BF16),
            pltpu.VMEM((wide + 2, 8, 16, 256), BF16),
            pltpu.VMEM((768, 256), BF16),
            pltpu.VMEM((512, 256), BF16),
            pltpu.VMEM((8, 16, 256), BF16),
            pltpu.VMEM((slots * planes, 8, 128), F32),
            pltpu.VMEM((own, 8, 128), F32),
            pltpu.VMEM((1024, 1024), BF16),
        ],
        compiler_params=pltpu.CompilerParams(vmem_limit_bytes=48 * 1024 * 1024),
    )(origin, x, footprint, lanes, sw, sb, cw)


MESH = pl.DeviceIdType.MESH


def meet(peers):
    barrier = pltpu.get_barrier_semaphore()
    for peer in peers:
        pl.semaphore_signal(barrier, inc=1, device_id=peer, device_id_type=MESH)
    pl.semaphore_wait(barrier, len(peers))


def slot_base(group, fields, slots, tiles):
    return jnp.clip(group * fields - 1, 0, tiles - slots)


def gather(fields, groups, *refs):
    cube, parts, x_out, part_outs = refs[0], refs[1:4], refs[4], refs[5:8]
    send_x, recv_x, send_w, recv_w, local = refs[8:]
    slots = x_out.shape[0]
    segments, tiles = part_outs[0].shape[0], fields * groups
    tile, segment = lax.axis_index("tile"), lax.axis_index("segment")
    group = tile // fields
    base = slot_base(group, fields, slots, tiles)
    mine = tile - base

    def remote(src, dst, send, recv, peer):
        return pltpu.make_async_remote_copy(
            src_ref=src,
            dst_ref=dst,
            send_sem=send,
            recv_sem=recv,
            device_id=peer,
            device_id_type=MESH,
        )

    others = [{"tile": (tile + k) % tiles} for k in range(1, tiles)]
    across = [{"segment": (segment + k) % segments} for k in range(1, segments)]
    meet(others + across)

    def plane_copy(row, target, i):
        other = target * fields + i
        slot = tile - slot_base(target, fields, slots, tiles)
        safe = jnp.clip(slot, 0, slots - 1)
        wanted = (target >= 0) & (target < groups) & (slot >= 0) & (slot < slots)
        copy = remote(
            cube.at[segment * fields + i],
            x_out.at[safe],
            send_x.at[row, i],
            recv_x.at[safe],
            {"tile": jnp.clip(other, 0, tiles - 1)},
        )
        return wanted & (other != tile), copy

    sends = [plane_copy(0, group, i) for i in range(fields)]
    if groups > 1:
        sends += [plane_copy(1, group + 1, i) for i in range(fields)]
        sends += [plane_copy(2, group - 1, i) for i in range(fields)]
    for wanted, copy in sends:
        pl.when(wanted)(copy.start)
    weights = [
        remote(parts[a], part_outs[a].at[segment], send_w.at[a, k], recv_w.at[a, segment], peer)
        for a in range(3)
        for k, peer in enumerate(across)
    ]
    for copy in weights:
        copy.start()
    own = [pltpu.make_async_copy(cube.at[segment * fields + tile % fields], x_out.at[mine], local.at[3])]
    own += [pltpu.make_async_copy(parts[a], part_outs[a].at[segment], local.at[a]) for a in range(3)]
    for copy in own:
        copy.start()

    for slot in range(slots):
        arriving = remote(cube.at[0], x_out.at[slot], send_x.at[0, 0], recv_x.at[slot], others[0])
        pl.when(mine != slot)(arriving.wait_recv)
    for a in range(3):
        for k in range(1, segments):
            source = (segment + k) % segments
            remote(
                parts[a], part_outs[a].at[source], send_w.at[a, 0], recv_w.at[a, source], across[0]
            ).wait_recv()
    for copy in own:
        copy.wait()
    for copy in weights:
        copy.wait_send()
    for wanted, copy in sends:
        pl.when(wanted)(copy.wait_send)


def scatter(fields, scores, out, send, recv, local):
    tile = lax.axis_index("tile")
    first, member = tile // fields * fields, tile % fields
    peers = [(member + k) % fields for k in range(1, fields)]
    meet([{"tile": first + peer} for peer in peers])

    def copy_to(k, peer, slot):
        return pltpu.make_async_remote_copy(
            src_ref=scores.at[peer],
            dst_ref=out.at[slot],
            send_sem=send.at[k],
            recv_sem=recv.at[slot],
            device_id={"tile": first + peer},
            device_id_type=MESH,
        )

    sends = [copy_to(k, peer, member) for k, peer in enumerate(peers)]
    for copy in sends:
        copy.start()
    own = pltpu.make_async_copy(scores.at[member], out.at[member], local)
    own.start()
    for k, peer in enumerate(peers):
        copy_to(k, peer, peer).wait_recv()
    own.wait()
    for copy in sends:
        copy.wait_send()


def per_device(
    cube,
    footprint,
    lift_weight,
    lift_bias,
    spatial_weight,
    spatial_bias,
    spectral_weight,
    head_weight,
):
    micro, planes, pixels = cube.shape
    segments = lax.axis_size("segment")
    tiles = lax.axis_size("tile")
    segment = lax.axis_index("segment")
    tile = lax.axis_index("tile")
    fields = micro // segments
    groups = tiles // fields
    own = planes * fields
    layers = spatial_weight.shape[0] * segments
    reach = layers if groups > 1 else 0
    assert reach <= planes
    wide = own + reach * min(2, groups - 1)
    slots = fields + min(2, groups - 1)

    hbm = pl.BlockSpec(memory_space=pl.ANY)
    dma = pltpu.SemaphoreType.DMA
    parts = (spatial_weight, spatial_bias, spectral_weight)
    x, sw, sb, cw = pl.pallas_call(
        functools.partial(gather, fields, groups),
        out_shape=[jax.ShapeDtypeStruct((slots, planes, pixels), F32)]
        + [jax.ShapeDtypeStruct((segments,) + part.shape, part.dtype) for part in parts],
        in_specs=[hbm] * 4,
        out_specs=[hbm] * 4,
        scratch_shapes=[
            dma((3, fields)),
            dma((slots,)),
            dma((3, segments)),
            dma((3, segments)),
            dma((4,)),
        ],
        compiler_params=pltpu.CompilerParams(collective_id=0, has_side_effects=True),
    )(cube, *parts)

    first = (tile // fields) * own
    begin = jnp.clip(first - reach, 0, tiles * planes - wide)
    skip = begin - slot_base(tile // fields, fields, slots, tiles) * planes
    origin = jnp.stack([first - begin, skip, segment * fields + tile % fields]).astype(jnp.int32)
    lanes = jnp.tile(jnp.stack([lift_weight, lift_bias, head_weight]), (1, 8))
    scores = run_network(
        own,
        reach,
        wide,
        origin,
        x,
        footprint,
        lanes,
        sw.reshape((layers,) + sw.shape[2:]),
        sb,
        cw.reshape((layers,) + cw.shape[2:]),
    )
    return pl.pallas_call(
        functools.partial(scatter, fields),
        out_shape=jax.ShapeDtypeStruct((fields, planes, pixels), F32),
        in_specs=[hbm],
        out_specs=hbm,
        scratch_shapes=[dma((fields,)), dma((fields,)), dma(())],
        compiler_params=pltpu.CompilerParams(collective_id=1, has_side_effects=True),
    )(scores)


def solution(mesh):
    placed = (
        P(None, "tile", None),
        P(),
        P(),
        P(),
        P("segment", None, None),
        P("segment", None),
        P("segment", None, None),
        P(),
    )
    return jax.shard_map(
        per_device,
        mesh=mesh,
        in_specs=placed,
        out_specs=P("segment", "tile", None),
        check_vma=False,
    )
```

```python
import functools

import jax
import jax.numpy as jnp
from jax import lax
from jax.experimental import pallas as pl
from jax.experimental.pallas import tpu as pltpu
from jax.sharding import PartitionSpec as P

SKY = 32
STEP = 4
CH = 32
F32 = jnp.float32
BF16 = jnp.bfloat16
HALF0 = [(0, y) for y in (0, 1, 2, 3)]
HALF1 = [(1, y) for y in (2, 3, 0, 1)]
OUT_POS = HALF0 + HALF1
IN_POS = (
    OUT_POS
    + [(-1, y) for y in (2, 3, 0, 1)]
    + [(2, y) for y in (0, 1, 2, 3)]
    + [(0, 4), (1, -1), (1, 4), (0, -1)]
    + [(2, 4), (-1, -1), (-1, 4), (2, -1)]
)


def dot(a, b, dims=((1,), (0,))):
    return lax.dot_general(a, b, (dims, ((), ())), preferred_element_type=F32)


def lane_block(shape):
    return lax.broadcasted_iota(jnp.int32, shape, len(shape) - 1) // CH


def split2(x):
    hi = x.astype(BF16)
    return hi, (x - hi.astype(F32)).astype(BF16)


def shift_rows(x, amount, group):
    row = lax.broadcasted_iota(jnp.int32, x.shape, 1)
    moved = pltpu.roll(x.astype(F32), amount % 16, axis=1)
    at = (row % group) - amount
    return jnp.where((at >= 0) & (at < group), moved, 0.0).astype(BF16)


def windows(hb):
    n = hb.shape[0]
    hb = hb.reshape(n, 2, 4, 16, 256)
    half0, half1 = hb[..., :128], hb[..., 128:]
    blk = lane_block((16, 128))[None, None, None]
    outer = jnp.broadcast_to((blk == 0) | (blk == 3), half0.shape)
    edge = jnp.where(outer, half0, half1)

    def shifted(part, amount, group):
        lead = part.shape[:-2]
        flat = part.reshape((-1, 16, 128))
        return shift_rows(flat, amount, group).reshape(lead + (16, 128))

    above = jnp.concatenate([shifted(edge[:, 1:2], 4, 16), edge[:, 0:1]], axis=1)
    below = jnp.concatenate([edge[:, 1:2], shifted(edge[:, 0:1], -4, 16)], axis=1)
    top = jnp.broadcast_to((blk == 1) | (blk == 3), half0.shape)
    rim = jnp.where(top, above, below)

    def from_left(part):
        return jnp.concatenate([shifted(part[:, :, 3:4], 1, 4), part[:, :, 0:3]], axis=2)

    def from_right(part):
        return jnp.concatenate([part[:, :, 1:4], shifted(part[:, :, 0:1], -1, 4)], axis=2)

    corner = jnp.where(outer, from_right(rim), from_left(rim))
    pieces = [half0, half1, from_left(half1), from_right(half0), rim, corner]
    return jnp.concatenate([p.reshape(n * 128, 128) for p in pieces], axis=1)


def network(
    own,
    reach,
    wide,
    origin_ref,
    footprint_ref,
    lanes_ref,
    x_hbm,
    sw_hbm,
    sb_hbm,
    cw_hbm,
    out_ref,
    h_ref,
    g_ref,
    w1_ref,
    w2_ref,
    k_ref,
    xs_ref,
    os_ref,
    perm_ref,
    x_ref,
    sw_ref,
    sb_ref,
    cw_ref,
    loaded,
):
    loads = [
        pltpu.make_async_copy(src, dst, loaded.at[n])
        for n, (src, dst) in enumerate(
            [(x_hbm, x_ref), (sw_hbm, sw_ref), (sb_hbm, sb_ref), (cw_hbm, cw_ref)]
        )
    ]
    for load in loads:
        load.start()
    layers = sw_ref.shape[0]
    depth = sb_ref.shape[1]
    sides = (wide - own) // reach if reach else 0
    offset, skip, member = origin_ref[0], origin_ref[1], origin_ref[2]

    q = lax.broadcasted_iota(jnp.int32, (8, 1024), 1)
    nb, r = q // 128, q % 128
    x2 = nb // 4
    y = (r // 4) % 4 * 8 + r // 64 * 4 + (nb % 4 + 2 * x2) % 4
    p = y * SKY + r % 4 * 8 + (r // 16) % 4 * 2 + x2
    at = lax.broadcasted_iota(jnp.int32, (1024, 1024), 0)
    perm_ref[...] = jnp.where(p[0:1] == at, 1.0, 0.0).astype(BF16)

    for load in loads:
        load.wait()
    x = jnp.concatenate([x_ref[s].astype(F32) for s in range(x_ref.shape[0])], axis=0)
    xp = dot(x.astype(BF16), perm_ref[...])
    for j in range(8):
        xs_ref[:, j, :] = xp[:, j * 128 : (j + 1) * 128]
    keep = footprint_ref[pl.ds(member, 1), :].astype(F32)
    kp = dot(jnp.broadcast_to(keep, (16, 1024)).astype(BF16), perm_ref[...])
    expand = jnp.where(
        lane_block((8, 256)) == lax.broadcasted_iota(jnp.int32, (8, 256), 0), 1.0, 0.0
    ).astype(BF16)
    k8 = jnp.concatenate([kp[0:1, j * 128 : (j + 1) * 128] for j in range(8)], axis=0)
    k_ref[...] = dot(k8.T.astype(BF16), expand).astype(BF16).reshape(8, 16, 256)

    lift_w, lift_b = lanes_ref[0:1, :], lanes_ref[1:2, :]

    def lift(f, _):
        full = dot(xs_ref[skip + f].T.astype(BF16), expand)
        fresh = (lift_w * full + lift_b).astype(BF16).reshape(8, 16, 256)
        h_ref[f] = fresh * k_ref[...]
        return 0

    lax.fori_loop(0, wide, lift, 0, unroll=4)
    g_ref[0] = jnp.zeros(g_ref.shape[1:], BF16)
    g_ref[wide + 1] = jnp.zeros(g_ref.shape[1:], BF16)

    spread = jnp.where(
        lax.broadcasted_iota(jnp.int32, (CH, 256), 1) % CH
        == lax.broadcasted_iota(jnp.int32, (CH, 256), 0),
        1.0,
        0.0,
    ).astype(BF16)
    block = lane_block((CH, 256))

    def layer_step(layer, _):
        taps = (0.5 * dot(sw_ref[layer].astype(F32).T.astype(BF16), spread)).astype(BF16)
        for kb, (xi, yi) in enumerate(IN_POS):
            rows = jnp.zeros((CH, 256), BF16)
            for nb, (xo, yo) in enumerate(OUT_POS):
                a, b = yi - yo, xi - xo
                if abs(a) <= 1 and abs(b) <= 1:
                    tap = (a + 1) * 3 + b + 1
                    rows = jnp.where(block == nb, taps[tap * CH : (tap + 1) * CH], rows)
            w1_ref[kb * CH : (kb + 1) * CH, :] = rows
        taps = dot(cw_ref[layer].astype(F32).T.astype(BF16), spread).astype(BF16)
        for kf in range(4):
            for kpos in range(4):
                rows = jnp.zeros((CH, 256), BF16)
                for nf in range(2):
                    tap = kf - nf
                    if 0 <= tap <= 2:
                        rows = jnp.where(
                            block == nf * 4 + kpos, taps[tap * CH : (tap + 1) * CH], rows
                        )
                kb = kf * 4 + kpos
                w2_ref[kb * CH : (kb + 1) * CH, :] = rows
        rows = sb_ref[layer // depth].astype(F32)
        here = lax.broadcasted_iota(jnp.int32, rows.shape, 0) == layer % depth
        row = jnp.sum(jnp.where(here, rows, 0.0), axis=0, keepdims=True)
        bias = 0.5 * dot(jnp.broadcast_to(row, (16, CH)).astype(BF16), spread)[0:1]

        left = reach - layer if reach else 0
        count = own + sides * left
        count = (count + STEP - 1) // STEP * STEP
        start = jnp.minimum(jnp.maximum(offset - left, 0), wide - count)
        steps = count // STEP

        def gate(f):
            t = (dot(windows(h_ref[pl.ds(f, STEP)]), w1_ref[...]) + bias).astype(BF16)
            return (t + t * jnp.tanh(t)).reshape(STEP, 8, 16, 256)

        def mix(f):
            gb = g_ref[pl.ds(f, STEP + 2)]
            halves = [
                jnp.concatenate(
                    [
                        gb[n + k, :, :, s * 128 : (s + 1) * 128].reshape(128, 128)
                        for k in range(4)
                    ],
                    axis=1,
                )
                for n in range(0, STEP, 2)
                for s in range(2)
            ]
            v = dot(jnp.concatenate(halves, axis=0), w2_ref[...])
            planes = [
                jnp.concatenate(
                    [
                        v[(n + s) * 128 : (n + s + 1) * 128, m * 128 : (m + 1) * 128]
                        for s in range(2)
                    ],
                    axis=1,
                )
                for n in range(0, STEP, 2)
                for m in range(2)
            ]
            v = jnp.stack(planes).reshape(STEP, 8, 16, 256).astype(BF16)
            half = jnp.asarray(0.5, BF16)
            return (half * h_ref[pl.ds(f, STEP)] + v) * k_ref[...][None]

        def put_gate(i):
            f = start + STEP * i
            g_ref[pl.ds(f + 1, STEP)] = gate(f)

        def put_mix(i):
            f = start + STEP * i
            h_ref[pl.ds(f, STEP)] = mix(f)

        def both(i, _):
            f, f2 = start + STEP * i, start + STEP * (i - 2)
            new_h = mix(f2)
            new_g = gate(f)
            h_ref[pl.ds(f2, STEP)] = new_h
            g_ref[pl.ds(f + 1, STEP)] = new_g
            return 0

        put_gate(0)
        put_gate(1)
        lax.fori_loop(2, steps, both, 0)
        put_mix(steps - 2)
        put_mix(steps - 1)
        return 0

    lax.fori_loop(0, layers, layer_step, 0)

    head = jnp.where(
        lane_block((8, 256)) == lax.broadcasted_iota(jnp.int32, (8, 256), 0), lanes_ref[2:3, :], 0.0
    )
    head_hi, head_lo = split2(head)
    heads = jnp.concatenate([head_hi.astype(F32), head_lo.astype(F32)], axis=0).astype(BF16)

    def score(f, _):
        both_parts = dot(heads, h_ref[offset + f].reshape(128, 256), ((1,), (1,)))
        os_ref[f] = both_parts[0:8] + both_parts[8:16]
        return 0

    lax.fori_loop(0, own, score, 0, unroll=4)
    tiled = jnp.concatenate([os_ref[:, j, :] for j in range(8)], axis=1)
    scores = dot(tiled.astype(BF16), perm_ref[...], ((1,), (1,)))
    planes = out_ref.shape[1]
    for s in range(out_ref.shape[0]):
        out_ref[s] = scores[s * planes : (s + 1) * planes].astype(BF16)


def run_network(own, reach, wide, origin, x, footprint, lanes, sw, sb, cw):
    slots, planes = x.shape[:2]
    vmem, hbm = pl.BlockSpec(memory_space=pltpu.VMEM), pl.BlockSpec(memory_space=pl.ANY)
    return pl.pallas_call(
        functools.partial(network, own, reach, wide),
        out_shape=jax.ShapeDtypeStruct((own // planes, planes, 1024), BF16),
        in_specs=[pl.BlockSpec(memory_space=pltpu.SMEM)] + [vmem] * 2 + [hbm] * 4,
        out_specs=vmem,
        scratch_shapes=[
            pltpu.VMEM((wide, 8, 16, 256), BF16),
            pltpu.VMEM((wide + 2, 8, 16, 256), BF16),
            pltpu.VMEM((768, 256), BF16),
            pltpu.VMEM((512, 256), BF16),
            pltpu.VMEM((8, 16, 256), BF16),
            pltpu.VMEM((slots * planes, 8, 128), F32),
            pltpu.VMEM((own, 8, 128), F32),
            pltpu.VMEM((1024, 1024), BF16),
        ]
        + [pltpu.VMEM(part.shape, part.dtype) for part in (x, sw, sb, cw)]
        + [pltpu.SemaphoreType.DMA((4,))],
        compiler_params=pltpu.CompilerParams(vmem_limit_bytes=48 * 1024 * 1024),
    )(origin, footprint, lanes, x, sw, sb, cw)


MESH = pl.DeviceIdType.MESH


def meet(peers):
    barrier = pltpu.get_barrier_semaphore()
    for peer in peers:
        pl.semaphore_signal(barrier, inc=1, device_id=peer, device_id_type=MESH)
    pl.semaphore_wait(barrier, len(peers))


def slot_base(group, fields, slots, tiles):
    return jnp.clip(group * fields - 1, 0, tiles - slots)


def gather(fields, groups, *refs):
    cube, parts, x_out, part_outs = refs[0], refs[1:4], refs[4], refs[5:8]
    send_x, recv_x, send_w, recv_w, local = refs[8:]
    slots = x_out.shape[0]
    segments, tiles = part_outs[0].shape[0], fields * groups
    tile, segment = lax.axis_index("tile"), lax.axis_index("segment")
    group = tile // fields
    base = slot_base(group, fields, slots, tiles)
    mine = tile - base

    def remote(src, dst, send, recv, peer):
        return pltpu.make_async_remote_copy(
            src_ref=src,
            dst_ref=dst,
            send_sem=send,
            recv_sem=recv,
            device_id=peer,
            device_id_type=MESH,
        )

    others = [{"tile": (tile + k) % tiles} for k in range(1, tiles)]
    across = [{"segment": (segment + k) % segments} for k in range(1, segments)]
    meet(others + across)

    def plane_copy(row, target, i):
        other = target * fields + i
        slot = tile - slot_base(target, fields, slots, tiles)
        safe = jnp.clip(slot, 0, slots - 1)
        wanted = (target >= 0) & (target < groups) & (slot >= 0) & (slot < slots)
        copy = remote(
            cube.at[i],
            x_out.at[safe],
            send_x.at[row, i],
            recv_x.at[safe],
            {"tile": jnp.clip(other, 0, tiles - 1)},
        )
        return wanted & (other != tile), copy

    sends = [plane_copy(0, group, i) for i in range(fields)]
    if groups > 1:
        sends += [plane_copy(1, group + 1, i) for i in range(fields)]
        sends += [plane_copy(2, group - 1, i) for i in range(fields)]
    for wanted, copy in sends:
        pl.when(wanted)(copy.start)
    weights = [
        remote(parts[a], part_outs[a].at[segment], send_w.at[a, k], recv_w.at[a, segment], peer)
        for a in range(3)
        for k, peer in enumerate(across)
    ]
    for copy in weights:
        copy.start()
    own = [pltpu.make_async_copy(cube.at[tile % fields], x_out.at[mine], local.at[3])]
    own += [pltpu.make_async_copy(parts[a], part_outs[a].at[segment], local.at[a]) for a in range(3)]
    for copy in own:
        copy.start()

    for slot in range(slots):
        arriving = remote(cube.at[0], x_out.at[slot], send_x.at[0, 0], recv_x.at[slot], others[0])
        pl.when(mine != slot)(arriving.wait_recv)
    for a in range(3):
        for k in range(1, segments):
            source = (segment + k) % segments
            remote(
                parts[a], part_outs[a].at[source], send_w.at[a, 0], recv_w.at[a, source], across[0]
            ).wait_recv()
    for copy in own:
        copy.wait()
    for copy in weights:
        copy.wait_send()
    for wanted, copy in sends:
        pl.when(wanted)(copy.wait_send)


def scatter(fields, scores, out, send, recv, local):
    tile = lax.axis_index("tile")
    first, member = tile // fields * fields, tile % fields
    peers = [(member + k) % fields for k in range(1, fields)]
    meet([{"tile": first + peer} for peer in peers])

    def copy_to(k, peer, slot):
        return pltpu.make_async_remote_copy(
            src_ref=scores.at[peer],
            dst_ref=out.at[slot],
            send_sem=send.at[k],
            recv_sem=recv.at[slot],
            device_id={"tile": first + peer},
            device_id_type=MESH,
        )

    sends = [copy_to(k, peer, member) for k, peer in enumerate(peers)]
    for copy in sends:
        copy.start()
    own = pltpu.make_async_copy(scores.at[member], out.at[member], local)
    own.start()
    for k, peer in enumerate(peers):
        copy_to(k, peer, peer).wait_recv()
    own.wait()
    for copy in sends:
        copy.wait_send()


def per_device(
    cube,
    footprint,
    lift_weight,
    lift_bias,
    spatial_weight,
    spatial_bias,
    spectral_weight,
    head_weight,
):
    micro, planes, pixels = cube.shape
    segments = lax.axis_size("segment")
    tiles = lax.axis_size("tile")
    segment = lax.axis_index("segment")
    tile = lax.axis_index("tile")
    fields = micro // segments
    groups = tiles // fields
    own = planes * fields
    layers = spatial_weight.shape[0] * segments
    reach = layers if groups > 1 else 0
    assert reach <= planes
    wide = own + reach * min(2, groups - 1)
    slots = fields + min(2, groups - 1)

    hbm = pl.BlockSpec(memory_space=pl.ANY)
    dma = pltpu.SemaphoreType.DMA
    mine = lax.dynamic_slice_in_dim(cube, segment * fields, fields, 0).astype(BF16)
    parts = (spatial_weight, spatial_bias, spectral_weight)
    x, sw, sb, cw = pl.pallas_call(
        functools.partial(gather, fields, groups),
        out_shape=[jax.ShapeDtypeStruct((slots, planes, pixels), BF16)]
        + [jax.ShapeDtypeStruct((segments,) + part.shape, part.dtype) for part in parts],
        in_specs=[hbm] * 4,
        out_specs=[hbm] * 4,
        scratch_shapes=[
            dma((3, fields)),
            dma((slots,)),
            dma((3, segments)),
            dma((3, segments)),
            dma((4,)),
        ],
        compiler_params=pltpu.CompilerParams(collective_id=0, has_side_effects=True),
    )(mine, *parts)

    first = (tile // fields) * own
    begin = jnp.clip(first - reach, 0, tiles * planes - wide)
    skip = begin - slot_base(tile // fields, fields, slots, tiles) * planes
    origin = jnp.stack([first - begin, skip, segment * fields + tile % fields]).astype(jnp.int32)
    lanes = jnp.tile(jnp.stack([lift_weight, lift_bias, head_weight]), (1, 8))
    scores = run_network(
        own,
        reach,
        wide,
        origin,
        x,
        footprint,
        lanes,
        sw.reshape((layers,) + sw.shape[2:]),
        sb,
        cw.reshape((layers,) + cw.shape[2:]),
    )
    mixed = pl.pallas_call(
        functools.partial(scatter, fields),
        out_shape=jax.ShapeDtypeStruct((fields, planes, pixels), BF16),
        in_specs=[hbm],
        out_specs=hbm,
        scratch_shapes=[dma((fields,)), dma((fields,)), dma(())],
        compiler_params=pltpu.CompilerParams(collective_id=1, has_side_effects=True),
    )(scores)
    return mixed.astype(F32)


def solution(mesh):
    placed = (
        P(None, "tile", None),
        P(),
        P(),
        P(),
        P("segment", None, None),
        P("segment", None),
        P("segment", None, None),
        P(),
    )
    return jax.shard_map(
        per_device,
        mesh=mesh,
        in_specs=placed,
        out_specs=P("segment", "tile", None),
        check_vma=False,
    )
```

```python
import functools

import jax
import jax.numpy as jnp
from jax import lax
from jax.experimental import pallas as pl
from jax.experimental.pallas import tpu as pltpu
from jax.sharding import PartitionSpec as P

SKY = 32
STEP = 8
CH = 32
F32 = jnp.float32
BF16 = jnp.bfloat16
HALF0 = [(0, y) for y in (0, 1, 2, 3)]
HALF1 = [(1, y) for y in (2, 3, 0, 1)]
OUT_POS = HALF0 + HALF1
IN_POS = (
    OUT_POS
    + [(-1, y) for y in (2, 3, 0, 1)]
    + [(2, y) for y in (0, 1, 2, 3)]
    + [(0, 4), (1, -1), (1, 4), (0, -1)]
    + [(2, 4), (-1, -1), (-1, 4), (2, -1)]
)


def dot(a, b, dims=((1,), (0,))):
    return lax.dot_general(a, b, (dims, ((), ())), preferred_element_type=F32)


def lane_block(shape):
    return lax.broadcasted_iota(jnp.int32, shape, len(shape) - 1) // CH


def split2(x):
    hi = x.astype(BF16)
    return hi, (x - hi.astype(F32)).astype(BF16)


def shift_rows(x, amount, group):
    row = lax.broadcasted_iota(jnp.int32, x.shape, 1)
    moved = pltpu.roll(x.astype(F32), amount % 16, axis=1)
    at = (row % group) - amount
    return jnp.where((at >= 0) & (at < group), moved, 0.0).astype(BF16)


def windows(hb):
    n = hb.shape[0]
    hb = hb.reshape(n, 2, 4, 16, 256)
    half0, half1 = hb[..., :128], hb[..., 128:]
    blk = lane_block((16, 128))[None, None, None]
    outer = jnp.broadcast_to((blk == 0) | (blk == 3), half0.shape)
    edge = jnp.where(outer, half0, half1)

    def shifted(part, amount, group):
        lead = part.shape[:-2]
        flat = part.reshape((-1, 16, 128))
        return shift_rows(flat, amount, group).reshape(lead + (16, 128))

    above = jnp.concatenate([shifted(edge[:, 1:2], 4, 16), edge[:, 0:1]], axis=1)
    below = jnp.concatenate([edge[:, 1:2], shifted(edge[:, 0:1], -4, 16)], axis=1)
    top = jnp.broadcast_to((blk == 1) | (blk == 3), half0.shape)
    rim = jnp.where(top, above, below)

    def from_left(part):
        return jnp.concatenate([shifted(part[:, :, 3:4], 1, 4), part[:, :, 0:3]], axis=2)

    def from_right(part):
        return jnp.concatenate([part[:, :, 1:4], shifted(part[:, :, 0:1], -1, 4)], axis=2)

    corner = jnp.where(outer, from_right(rim), from_left(rim))
    pieces = [half0, half1, from_left(half1), from_right(half0), rim, corner]
    return jnp.concatenate([p.reshape(n * 128, 128) for p in pieces], axis=1)


def network(
    own,
    reach,
    wide,
    origin_ref,
    footprint_ref,
    lanes_ref,
    x_ref,
    sw_ref,
    sb_ref,
    cw_ref,
    out_ref,
    h_ref,
    g_ref,
    w1_ref,
    w2_ref,
    k_ref,
    xs_ref,
    os_ref,
    perm_ref,
):
    layers = sw_ref.shape[0]
    depth = sb_ref.shape[1]
    sides = (wide - own) // reach if reach else 0
    offset, skip, member = origin_ref[0], origin_ref[1], origin_ref[2]

    q = lax.broadcasted_iota(jnp.int32, (8, 1024), 1)
    nb, r = q // 128, q % 128
    x2 = nb // 4
    y = (r // 4) % 4 * 8 + r // 64 * 4 + (nb % 4 + 2 * x2) % 4
    p = y * SKY + r % 4 * 8 + (r // 16) % 4 * 2 + x2
    at = lax.broadcasted_iota(jnp.int32, (1024, 1024), 0)
    perm_ref[...] = jnp.where(p[0:1] == at, 1.0, 0.0).astype(BF16)

    x = jnp.concatenate([x_ref[s].astype(F32) for s in range(x_ref.shape[0])], axis=0)
    xp = dot(x.astype(BF16), perm_ref[...])
    for j in range(8):
        xs_ref[:, j, :] = xp[:, j * 128 : (j + 1) * 128]
    keep = footprint_ref[pl.ds(member, 1), :].astype(F32)
    kp = dot(jnp.broadcast_to(keep, (16, 1024)).astype(BF16), perm_ref[...])
    expand = jnp.where(
        lane_block((8, 256)) == lax.broadcasted_iota(jnp.int32, (8, 256), 0), 1.0, 0.0
    ).astype(BF16)
    k8 = jnp.concatenate([kp[0:1, j * 128 : (j + 1) * 128] for j in range(8)], axis=0)
    k_ref[...] = dot(k8.T.astype(BF16), expand).astype(BF16).reshape(8, 16, 256)

    lift_w, lift_b = lanes_ref[0:1, :], lanes_ref[1:2, :]

    def lift(f, _):
        full = dot(xs_ref[skip + f].T.astype(BF16), expand)
        fresh = (lift_w * full + lift_b).astype(BF16).reshape(8, 16, 256)
        h_ref[f] = fresh * k_ref[...]
        return 0

    lax.fori_loop(0, wide, lift, 0, unroll=4)
    g_ref[0] = jnp.zeros(g_ref.shape[1:], BF16)
    g_ref[wide + 1] = jnp.zeros(g_ref.shape[1:], BF16)

    spread = jnp.where(
        lax.broadcasted_iota(jnp.int32, (CH, 256), 1) % CH
        == lax.broadcasted_iota(jnp.int32, (CH, 256), 0),
        1.0,
        0.0,
    ).astype(BF16)
    block = lane_block((CH, 256))

    def layer_step(layer, _):
        taps = (0.5 * dot(sw_ref[layer].astype(F32).T.astype(BF16), spread)).astype(BF16)
        for kb, (xi, yi) in enumerate(IN_POS):
            rows = jnp.zeros((CH, 256), BF16)
            for nb, (xo, yo) in enumerate(OUT_POS):
                a, b = yi - yo, xi - xo
                if abs(a) <= 1 and abs(b) <= 1:
                    tap = (a + 1) * 3 + b + 1
                    rows = jnp.where(block == nb, taps[tap * CH : (tap + 1) * CH], rows)
            w1_ref[kb * CH : (kb + 1) * CH, :] = rows
        taps = dot(cw_ref[layer].astype(F32).T.astype(BF16), spread).astype(BF16)
        for kf in range(4):
            for kpos in range(4):
                rows = jnp.zeros((CH, 256), BF16)
                for nf in range(2):
                    tap = kf - nf
                    if 0 <= tap <= 2:
                        rows = jnp.where(
                            block == nf * 4 + kpos, taps[tap * CH : (tap + 1) * CH], rows
                        )
                kb = kf * 4 + kpos
                w2_ref[kb * CH : (kb + 1) * CH, :] = rows
        rows = sb_ref[layer // depth].astype(F32)
        here = lax.broadcasted_iota(jnp.int32, rows.shape, 0) == layer % depth
        row = jnp.sum(jnp.where(here, rows, 0.0), axis=0, keepdims=True)
        bias = 0.5 * dot(jnp.broadcast_to(row, (16, CH)).astype(BF16), spread)[0:1]

        left = reach - layer if reach else 0
        count = own + sides * left
        count = (count + STEP - 1) // STEP * STEP
        start = jnp.minimum(jnp.maximum(offset - left, 0), wide - count)
        steps = count // STEP

        def gate(f):
            t = (dot(windows(h_ref[pl.ds(f, STEP)]), w1_ref[...]) + bias).astype(BF16)
            return (t + t * jnp.tanh(t)).reshape(STEP, 8, 16, 256)

        def mix(f):
            gb = g_ref[pl.ds(f, STEP + 2)]
            halves = [
                jnp.concatenate(
                    [
                        gb[n + k, :, :, s * 128 : (s + 1) * 128].reshape(128, 128)
                        for k in range(4)
                    ],
                    axis=1,
                )
                for n in range(0, STEP, 2)
                for s in range(2)
            ]
            v = dot(jnp.concatenate(halves, axis=0), w2_ref[...])
            planes = [
                jnp.concatenate(
                    [
                        v[(n + s) * 128 : (n + s + 1) * 128, m * 128 : (m + 1) * 128]
                        for s in range(2)
                    ],
                    axis=1,
                )
                for n in range(0, STEP, 2)
                for m in range(2)
            ]
            v = jnp.stack(planes).reshape(STEP, 8, 16, 256).astype(BF16)
            half = jnp.asarray(0.5, BF16)
            return (half * h_ref[pl.ds(f, STEP)] + v) * k_ref[...][None]

        def put_gate(i):
            f = start + STEP * i
            g_ref[pl.ds(f + 1, STEP)] = gate(f)

        def put_mix(i):
            f = start + STEP * i
            h_ref[pl.ds(f, STEP)] = mix(f)

        def both(i, _):
            f, f2 = start + STEP * i, start + STEP * (i - 2)
            new_h = mix(f2)
            new_g = gate(f)
            h_ref[pl.ds(f2, STEP)] = new_h
            g_ref[pl.ds(f + 1, STEP)] = new_g
            return 0

        put_gate(0)
        put_gate(1)
        lax.fori_loop(2, steps, both, 0)
        put_mix(steps - 2)
        put_mix(steps - 1)
        return 0

    lax.fori_loop(0, layers, layer_step, 0)

    head = jnp.where(
        lane_block((8, 256)) == lax.broadcasted_iota(jnp.int32, (8, 256), 0), lanes_ref[2:3, :], 0.0
    )
    head_hi, head_lo = split2(head)
    heads = jnp.concatenate([head_hi.astype(F32), head_lo.astype(F32)], axis=0).astype(BF16)

    def score(f, _):
        both_parts = dot(heads, h_ref[offset + f].reshape(128, 256), ((1,), (1,)))
        os_ref[f] = both_parts[0:8] + both_parts[8:16]
        return 0

    lax.fori_loop(0, own, score, 0, unroll=4)
    tiled = jnp.concatenate([os_ref[:, j, :] for j in range(8)], axis=1)
    scores = dot(tiled.astype(BF16), perm_ref[...], ((1,), (1,)))
    planes = out_ref.shape[1]
    for s in range(out_ref.shape[0]):
        out_ref[s] = scores[s * planes : (s + 1) * planes].astype(BF16)


def run_network(own, reach, wide, origin, x, footprint, lanes, sw, sb, cw):
    slots, planes = x.shape[:2]
    vmem = pl.BlockSpec(memory_space=pltpu.VMEM)
    return pl.pallas_call(
        functools.partial(network, own, reach, wide),
        out_shape=jax.ShapeDtypeStruct((own // planes, planes, 1024), BF16),
        in_specs=[pl.BlockSpec(memory_space=pltpu.SMEM)] + [vmem] * 6,
        out_specs=vmem,
        scratch_shapes=[
            pltpu.VMEM((wide, 8, 16, 256), BF16),
            pltpu.VMEM((wide + 2, 8, 16, 256), BF16),
            pltpu.VMEM((768, 256), BF16),
            pltpu.VMEM((512, 256), BF16),
            pltpu.VMEM((8, 16, 256), BF16),
            pltpu.VMEM((slots * planes, 8, 128), F32),
            pltpu.VMEM((own, 8, 128), F32),
            pltpu.VMEM((1024, 1024), BF16),
        ],
        compiler_params=pltpu.CompilerParams(vmem_limit_bytes=48 * 1024 * 1024),
    )(origin, footprint, lanes, x, sw, sb, cw)


MESH = pl.DeviceIdType.MESH


def meet(peers):
    barrier = pltpu.get_barrier_semaphore()
    for peer in peers:
        pl.semaphore_signal(barrier, inc=1, device_id=peer, device_id_type=MESH)
    pl.semaphore_wait(barrier, len(peers))


def slot_base(group, fields, slots, tiles):
    return jnp.clip(group * fields - 1, 0, tiles - slots)


def gather(fields, groups, *refs):
    cube, parts, x_out, part_outs = refs[0], refs[1:4], refs[4], refs[5:8]
    send_x, recv_x, send_w, recv_w, local = refs[8:]
    slots = x_out.shape[0]
    segments, tiles = part_outs[0].shape[0], fields * groups
    tile, segment = lax.axis_index("tile"), lax.axis_index("segment")
    group = tile // fields
    base = slot_base(group, fields, slots, tiles)
    mine = tile - base

    def remote(src, dst, send, recv, peer):
        return pltpu.make_async_remote_copy(
            src_ref=src,
            dst_ref=dst,
            send_sem=send,
            recv_sem=recv,
            device_id=peer,
            device_id_type=MESH,
        )

    others = [{"tile": (tile + k) % tiles} for k in range(1, tiles)]
    across = [{"segment": (segment + k) % segments} for k in range(1, segments)]
    meet(others + across)

    def plane_copy(row, target, i):
        other = target * fields + i
        slot = tile - slot_base(target, fields, slots, tiles)
        safe = jnp.clip(slot, 0, slots - 1)
        wanted = (target >= 0) & (target < groups) & (slot >= 0) & (slot < slots)
        copy = remote(
            cube.at[i],
            x_out.at[safe],
            send_x.at[row, i],
            recv_x.at[safe],
            {"tile": jnp.clip(other, 0, tiles - 1)},
        )
        return wanted & (other != tile), copy

    sends = [plane_copy(0, group, i) for i in range(fields)]
    if groups > 1:
        sends += [plane_copy(1, group + 1, i) for i in range(fields)]
        sends += [plane_copy(2, group - 1, i) for i in range(fields)]
    for wanted, copy in sends:
        pl.when(wanted)(copy.start)
    weights = [
        remote(parts[a], part_outs[a].at[segment], send_w.at[a, k], recv_w.at[a, segment], peer)
        for a in range(3)
        for k, peer in enumerate(across)
    ]
    for copy in weights:
        copy.start()
    own = [pltpu.make_async_copy(cube.at[tile % fields], x_out.at[mine], local.at[3])]
    own += [pltpu.make_async_copy(parts[a], part_outs[a].at[segment], local.at[a]) for a in range(3)]
    for copy in own:
        copy.start()

    for slot in range(slots):
        arriving = remote(cube.at[0], x_out.at[slot], send_x.at[0, 0], recv_x.at[slot], others[0])
        pl.when(mine != slot)(arriving.wait_recv)
    for a in range(3):
        for k in range(1, segments):
            source = (segment + k) % segments
            remote(
                parts[a], part_outs[a].at[source], send_w.at[a, 0], recv_w.at[a, source], across[0]
            ).wait_recv()
    for copy in own:
        copy.wait()
    for copy in weights:
        copy.wait_send()
    for wanted, copy in sends:
        pl.when(wanted)(copy.wait_send)


def scatter(fields, scores, out, send, recv, local):
    tile = lax.axis_index("tile")
    first, member = tile // fields * fields, tile % fields
    peers = [(member + k) % fields for k in range(1, fields)]
    meet([{"tile": first + peer} for peer in peers])

    def copy_to(k, peer, slot):
        return pltpu.make_async_remote_copy(
            src_ref=scores.at[peer],
            dst_ref=out.at[slot],
            send_sem=send.at[k],
            recv_sem=recv.at[slot],
            device_id={"tile": first + peer},
            device_id_type=MESH,
        )

    sends = [copy_to(k, peer, member) for k, peer in enumerate(peers)]
    for copy in sends:
        copy.start()
    own = pltpu.make_async_copy(scores.at[member], out.at[member], local)
    own.start()
    for k, peer in enumerate(peers):
        copy_to(k, peer, peer).wait_recv()
    own.wait()
    for copy in sends:
        copy.wait_send()


def per_device(
    cube,
    footprint,
    lift_weight,
    lift_bias,
    spatial_weight,
    spatial_bias,
    spectral_weight,
    head_weight,
):
    micro, planes, pixels = cube.shape
    segments = lax.axis_size("segment")
    tiles = lax.axis_size("tile")
    segment = lax.axis_index("segment")
    tile = lax.axis_index("tile")
    fields = micro // segments
    groups = tiles // fields
    own = planes * fields
    layers = spatial_weight.shape[0] * segments
    reach = layers if groups > 1 else 0
    assert reach <= planes
    wide = own + reach * min(2, groups - 1)
    slots = fields + min(2, groups - 1)

    hbm, vmem = pl.BlockSpec(memory_space=pl.ANY), pl.BlockSpec(memory_space=pltpu.VMEM)
    dma = pltpu.SemaphoreType.DMA
    mine = lax.dynamic_slice_in_dim(cube, segment * fields, fields, 0).astype(BF16)
    parts = (spatial_weight, spatial_bias, spectral_weight)
    x, sw, sb, cw = pl.pallas_call(
        functools.partial(gather, fields, groups),
        out_shape=[jax.ShapeDtypeStruct((slots, planes, pixels), BF16)]
        + [jax.ShapeDtypeStruct((segments,) + part.shape, part.dtype) for part in parts],
        in_specs=[vmem] + [hbm] * 3,
        out_specs=[vmem] * 4,
        scratch_shapes=[
            dma((3, fields)),
            dma((slots,)),
            dma((3, segments)),
            dma((3, segments)),
            dma((4,)),
        ],
        compiler_params=pltpu.CompilerParams(collective_id=0, has_side_effects=True),
    )(mine, *parts)

    first = (tile // fields) * own
    begin = jnp.clip(first - reach, 0, tiles * planes - wide)
    skip = begin - slot_base(tile // fields, fields, slots, tiles) * planes
    origin = jnp.stack([first - begin, skip, segment * fields + tile % fields]).astype(jnp.int32)
    lanes = jnp.tile(jnp.stack([lift_weight, lift_bias, head_weight]), (1, 8))
    scores = run_network(
        own,
        reach,
        wide,
        origin,
        x,
        footprint,
        lanes,
        sw.reshape((layers,) + sw.shape[2:]),
        sb,
        cw.reshape((layers,) + cw.shape[2:]),
    )
    mixed = pl.pallas_call(
        functools.partial(scatter, fields),
        out_shape=jax.ShapeDtypeStruct((fields, planes, pixels), BF16),
        in_specs=[vmem],
        out_specs=vmem,
        scratch_shapes=[dma((fields,)), dma((fields,)), dma(())],
        compiler_params=pltpu.CompilerParams(collective_id=1, has_side_effects=True),
    )(scores)
    return mixed.astype(F32)


def solution(mesh):
    placed = (
        P(None, "tile", None),
        P(),
        P(),
        P(),
        P("segment", None, None),
        P("segment", None),
        P("segment", None, None),
        P(),
    )
    return jax.shard_map(
        per_device,
        mesh=mesh,
        in_specs=placed,
        out_specs=P("segment", "tile", None),
        check_vma=False,
    )
```

```python
import functools

import jax
import jax.numpy as jnp
from jax import lax
from jax.experimental import pallas as pl
from jax.experimental.pallas import tpu as pltpu
from jax.sharding import PartitionSpec as P

SKY = 32
STEP = 8
CH = 32
F32 = jnp.float32
BF16 = jnp.bfloat16
HALF0 = [(0, y) for y in (0, 1, 2, 3)]
HALF1 = [(1, y) for y in (2, 3, 0, 1)]
OUT_POS = HALF0 + HALF1
IN_POS = (
    OUT_POS
    + [(-1, y) for y in (2, 3, 0, 1)]
    + [(2, y) for y in (0, 1, 2, 3)]
    + [(0, 4), (1, -1), (1, 4), (0, -1)]
    + [(2, 4), (-1, -1), (-1, 4), (2, -1)]
)


def dot(a, b, dims=((1,), (0,))):
    return lax.dot_general(a, b, (dims, ((), ())), preferred_element_type=F32)


def lane_block(shape):
    return lax.broadcasted_iota(jnp.int32, shape, len(shape) - 1) // CH


def split2(x):
    hi = x.astype(BF16)
    return hi, (x - hi.astype(F32)).astype(BF16)


def shift_rows(x, amount, group):
    row = lax.broadcasted_iota(jnp.int32, x.shape, 1)
    moved = pltpu.roll(x.astype(F32), amount % 16, axis=1)
    at = (row % group) - amount
    return jnp.where((at >= 0) & (at < group), moved, 0.0).astype(BF16)


def windows(hb):
    n = hb.shape[0]
    hb = hb.reshape(n, 2, 4, 16, 256)
    half0, half1 = hb[..., :128], hb[..., 128:]
    blk = lane_block((16, 128))[None, None, None]
    outer = jnp.broadcast_to((blk == 0) | (blk == 3), half0.shape)
    edge = jnp.where(outer, half0, half1)

    def shifted(part, amount, group):
        lead = part.shape[:-2]
        flat = part.reshape((-1, 16, 128))
        return shift_rows(flat, amount, group).reshape(lead + (16, 128))

    above = jnp.concatenate([shifted(edge[:, 1:2], 4, 16), edge[:, 0:1]], axis=1)
    below = jnp.concatenate([edge[:, 1:2], shifted(edge[:, 0:1], -4, 16)], axis=1)
    top = jnp.broadcast_to((blk == 1) | (blk == 3), half0.shape)
    rim = jnp.where(top, above, below)

    def from_left(part):
        return jnp.concatenate([shifted(part[:, :, 3:4], 1, 4), part[:, :, 0:3]], axis=2)

    def from_right(part):
        return jnp.concatenate([part[:, :, 1:4], shifted(part[:, :, 0:1], -1, 4)], axis=2)

    corner = jnp.where(outer, from_right(rim), from_left(rim))
    pieces = [half0, half1, from_left(half1), from_right(half0), rim, corner]
    return jnp.concatenate([p.reshape(n * 128, 128) for p in pieces], axis=1)


def network(
    own,
    reach,
    wide,
    origin_ref,
    footprint_ref,
    lanes_ref,
    x_hbm,
    sw_hbm,
    sb_hbm,
    cw_hbm,
    out_ref,
    h_ref,
    g_ref,
    w1_ref,
    w2_ref,
    k_ref,
    xs_ref,
    os_ref,
    perm_ref,
    x_ref,
    sw_ref,
    sb_ref,
    cw_ref,
    loaded,
):
    loads = [
        pltpu.make_async_copy(src, dst, loaded.at[n])
        for n, (src, dst) in enumerate(
            [(x_hbm, x_ref), (sw_hbm, sw_ref), (sb_hbm, sb_ref), (cw_hbm, cw_ref)]
        )
    ]
    for load in loads:
        load.start()
    layers = sw_ref.shape[0]
    depth = sb_ref.shape[1]
    sides = (wide - own) // reach if reach else 0
    offset, skip, member = origin_ref[0], origin_ref[1], origin_ref[2]

    q = lax.broadcasted_iota(jnp.int32, (8, 1024), 1)
    nb, r = q // 128, q % 128
    x2 = nb // 4
    y = (r // 4) % 4 * 8 + r // 64 * 4 + (nb % 4 + 2 * x2) % 4
    p = y * SKY + r % 4 * 8 + (r // 16) % 4 * 2 + x2
    at = lax.broadcasted_iota(jnp.int32, (1024, 1024), 0)
    perm_ref[...] = jnp.where(p[0:1] == at, 1.0, 0.0).astype(BF16)

    for load in loads:
        load.wait()
    x = jnp.concatenate([x_ref[s].astype(F32) for s in range(x_ref.shape[0])], axis=0)
    xp = dot(x.astype(BF16), perm_ref[...])
    for j in range(8):
        xs_ref[:, j, :] = xp[:, j * 128 : (j + 1) * 128]
    keep = footprint_ref[pl.ds(member, 1), :].astype(F32)
    kp = dot(jnp.broadcast_to(keep, (16, 1024)).astype(BF16), perm_ref[...])
    expand = jnp.where(
        lane_block((8, 256)) == lax.broadcasted_iota(jnp.int32, (8, 256), 0), 1.0, 0.0
    ).astype(BF16)
    k8 = jnp.concatenate([kp[0:1, j * 128 : (j + 1) * 128] for j in range(8)], axis=0)
    k_ref[...] = dot(k8.T.astype(BF16), expand).astype(BF16).reshape(8, 16, 256)

    lift_w, lift_b = lanes_ref[0:1, :], lanes_ref[1:2, :]

    def lift(f, _):
        full = dot(xs_ref[skip + f].T.astype(BF16), expand)
        fresh = (lift_w * full + lift_b).astype(BF16).reshape(8, 16, 256)
        h_ref[f] = fresh * k_ref[...]
        return 0

    lax.fori_loop(0, wide, lift, 0, unroll=4)
    g_ref[0] = jnp.zeros(g_ref.shape[1:], BF16)
    g_ref[wide + 1] = jnp.zeros(g_ref.shape[1:], BF16)

    spread = jnp.where(
        lax.broadcasted_iota(jnp.int32, (CH, 256), 1) % CH
        == lax.broadcasted_iota(jnp.int32, (CH, 256), 0),
        1.0,
        0.0,
    ).astype(BF16)
    block = lane_block((CH, 256))

    def layer_step(layer, _):
        taps = (0.5 * dot(sw_ref[layer].astype(F32).T.astype(BF16), spread)).astype(BF16)
        for kb, (xi, yi) in enumerate(IN_POS):
            rows = jnp.zeros((CH, 256), BF16)
            for nb, (xo, yo) in enumerate(OUT_POS):
                a, b = yi - yo, xi - xo
                if abs(a) <= 1 and abs(b) <= 1:
                    tap = (a + 1) * 3 + b + 1
                    rows = jnp.where(block == nb, taps[tap * CH : (tap + 1) * CH], rows)
            w1_ref[kb * CH : (kb + 1) * CH, :] = rows
        taps = dot(cw_ref[layer].astype(F32).T.astype(BF16), spread).astype(BF16)
        for kf in range(4):
            for kpos in range(4):
                rows = jnp.zeros((CH, 256), BF16)
                for nf in range(2):
                    tap = kf - nf
                    if 0 <= tap <= 2:
                        rows = jnp.where(
                            block == nf * 4 + kpos, taps[tap * CH : (tap + 1) * CH], rows
                        )
                kb = kf * 4 + kpos
                w2_ref[kb * CH : (kb + 1) * CH, :] = rows
        rows = sb_ref[layer // depth].astype(F32)
        here = lax.broadcasted_iota(jnp.int32, rows.shape, 0) == layer % depth
        row = jnp.sum(jnp.where(here, rows, 0.0), axis=0, keepdims=True)
        bias = 0.5 * dot(jnp.broadcast_to(row, (16, CH)).astype(BF16), spread)[0:1]

        left = reach - layer if reach else 0
        count = own + sides * left
        count = (count + STEP - 1) // STEP * STEP
        start = jnp.minimum(jnp.maximum(offset - left, 0), wide - count)
        steps = count // STEP

        def gate(f):
            t = (dot(windows(h_ref[pl.ds(f, STEP)]), w1_ref[...]) + bias).astype(BF16)
            return (t + t * jnp.tanh(t)).reshape(STEP, 8, 16, 256)

        def mix(f):
            gb = g_ref[pl.ds(f, STEP + 2)]
            halves = [
                jnp.concatenate(
                    [
                        gb[n + k, :, :, s * 128 : (s + 1) * 128].reshape(128, 128)
                        for k in range(4)
                    ],
                    axis=1,
                )
                for n in range(0, STEP, 2)
                for s in range(2)
            ]
            v = dot(jnp.concatenate(halves, axis=0), w2_ref[...])
            planes = [
                jnp.concatenate(
                    [
                        v[(n + s) * 128 : (n + s + 1) * 128, m * 128 : (m + 1) * 128]
                        for s in range(2)
                    ],
                    axis=1,
                )
                for n in range(0, STEP, 2)
                for m in range(2)
            ]
            v = jnp.stack(planes).reshape(STEP, 8, 16, 256).astype(BF16)
            half = jnp.asarray(0.5, BF16)
            return (half * h_ref[pl.ds(f, STEP)] + v) * k_ref[...][None]

        def put_gate(i):
            f = start + STEP * i
            g_ref[pl.ds(f + 1, STEP)] = gate(f)

        def put_mix(i):
            f = start + STEP * i
            h_ref[pl.ds(f, STEP)] = mix(f)

        def both(i, _):
            f, f2 = start + STEP * i, start + STEP * (i - 2)
            new_h = mix(f2)
            new_g = gate(f)
            h_ref[pl.ds(f2, STEP)] = new_h
            g_ref[pl.ds(f + 1, STEP)] = new_g
            return 0

        put_gate(0)
        put_gate(1)
        lax.fori_loop(2, steps, both, 0)
        put_mix(steps - 2)
        put_mix(steps - 1)
        return 0

    lax.fori_loop(0, layers, layer_step, 0)

    head = jnp.where(
        lane_block((8, 256)) == lax.broadcasted_iota(jnp.int32, (8, 256), 0), lanes_ref[2:3, :], 0.0
    )
    head_hi, head_lo = split2(head)
    heads = jnp.concatenate([head_hi.astype(F32), head_lo.astype(F32)], axis=0).astype(BF16)

    def score(f, _):
        both_parts = dot(heads, h_ref[offset + f].reshape(128, 256), ((1,), (1,)))
        os_ref[f] = both_parts[0:8] + both_parts[8:16]
        return 0

    lax.fori_loop(0, own, score, 0, unroll=4)
    tiled = jnp.concatenate([os_ref[:, j, :] for j in range(8)], axis=1)
    scores = dot(tiled.astype(BF16), perm_ref[...], ((1,), (1,)))
    planes = out_ref.shape[1]
    for s in range(out_ref.shape[0]):
        out_ref[s] = scores[s * planes : (s + 1) * planes].astype(BF16)


def run_network(own, reach, wide, origin, x, footprint, lanes, sw, sb, cw):
    slots, planes = x.shape[:2]
    vmem = pl.BlockSpec(memory_space=pltpu.VMEM)
    far = pl.BlockSpec(memory_space=pltpu.HBM)
    return pl.pallas_call(
        functools.partial(network, own, reach, wide),
        out_shape=jax.ShapeDtypeStruct((own // planes, planes, 1024), BF16),
        in_specs=[pl.BlockSpec(memory_space=pltpu.SMEM)] + [vmem] * 2 + [far] * 4,
        out_specs=vmem,
        scratch_shapes=[
            pltpu.VMEM((wide, 8, 16, 256), BF16),
            pltpu.VMEM((wide + 2, 8, 16, 256), BF16),
            pltpu.VMEM((768, 256), BF16),
            pltpu.VMEM((512, 256), BF16),
            pltpu.VMEM((8, 16, 256), BF16),
            pltpu.VMEM((slots * planes, 8, 128), F32),
            pltpu.VMEM((own, 8, 128), F32),
            pltpu.VMEM((1024, 1024), BF16),
        ]
        + [pltpu.VMEM(part.shape, part.dtype) for part in (x, sw, sb, cw)]
        + [pltpu.SemaphoreType.DMA((4,))],
        compiler_params=pltpu.CompilerParams(vmem_limit_bytes=48 * 1024 * 1024),
    )(origin, footprint, lanes, x, sw, sb, cw)


MESH = pl.DeviceIdType.MESH


def meet(peers):
    barrier = pltpu.get_barrier_semaphore()
    for peer in peers:
        pl.semaphore_signal(barrier, inc=1, device_id=peer, device_id_type=MESH)
    pl.semaphore_wait(barrier, len(peers))


def slot_base(group, fields, slots, tiles):
    return jnp.clip(group * fields - 1, 0, tiles - slots)


def gather(fields, groups, *refs):
    cube, parts, x_out, part_outs = refs[0], refs[1:4], refs[4], refs[5:8]
    send_x, recv_x, send_w, recv_w, local = refs[8:]
    slots = x_out.shape[0]
    segments, tiles = part_outs[0].shape[0], fields * groups
    tile, segment = lax.axis_index("tile"), lax.axis_index("segment")
    group = tile // fields
    base = slot_base(group, fields, slots, tiles)
    mine = tile - base

    def remote(src, dst, send, recv, peer):
        return pltpu.make_async_remote_copy(
            src_ref=src,
            dst_ref=dst,
            send_sem=send,
            recv_sem=recv,
            device_id=peer,
            device_id_type=MESH,
        )

    others = [{"tile": (tile + k) % tiles} for k in range(1, tiles)]
    across = [{"segment": (segment + k) % segments} for k in range(1, segments)]
    meet(others + across)

    def plane_copy(row, target, i):
        other = target * fields + i
        slot = tile - slot_base(target, fields, slots, tiles)
        safe = jnp.clip(slot, 0, slots - 1)
        wanted = (target >= 0) & (target < groups) & (slot >= 0) & (slot < slots)
        copy = remote(
            cube.at[i],
            x_out.at[safe],
            send_x.at[row, i],
            recv_x.at[safe],
            {"tile": jnp.clip(other, 0, tiles - 1)},
        )
        return wanted & (other != tile), copy

    sends = [plane_copy(0, group, i) for i in range(fields)]
    if groups > 1:
        sends += [plane_copy(1, group + 1, i) for i in range(fields)]
        sends += [plane_copy(2, group - 1, i) for i in range(fields)]
    for wanted, copy in sends:
        pl.when(wanted)(copy.start)
    weights = [
        remote(parts[a], part_outs[a].at[segment], send_w.at[a, k], recv_w.at[a, segment], peer)
        for a in range(3)
        for k, peer in enumerate(across)
    ]
    for copy in weights:
        copy.start()
    own = [pltpu.make_async_copy(cube.at[tile % fields], x_out.at[mine], local.at[3])]
    own += [pltpu.make_async_copy(parts[a], part_outs[a].at[segment], local.at[a]) for a in range(3)]
    for copy in own:
        copy.start()

    for slot in range(slots):
        arriving = remote(cube.at[0], x_out.at[slot], send_x.at[0, 0], recv_x.at[slot], others[0])
        pl.when(mine != slot)(arriving.wait_recv)
    for a in range(3):
        for k in range(1, segments):
            source = (segment + k) % segments
            remote(
                parts[a], part_outs[a].at[source], send_w.at[a, 0], recv_w.at[a, source], across[0]
            ).wait_recv()
    for copy in own:
        copy.wait()
    for copy in weights:
        copy.wait_send()
    for wanted, copy in sends:
        pl.when(wanted)(copy.wait_send)


def scatter(fields, scores, out, send, recv, local):
    tile = lax.axis_index("tile")
    first, member = tile // fields * fields, tile % fields
    peers = [(member + k) % fields for k in range(1, fields)]
    meet([{"tile": first + peer} for peer in peers])

    def copy_to(k, peer, slot):
        return pltpu.make_async_remote_copy(
            src_ref=scores.at[peer],
            dst_ref=out.at[slot],
            send_sem=send.at[k],
            recv_sem=recv.at[slot],
            device_id={"tile": first + peer},
            device_id_type=MESH,
        )

    sends = [copy_to(k, peer, member) for k, peer in enumerate(peers)]
    for copy in sends:
        copy.start()
    own = pltpu.make_async_copy(scores.at[member], out.at[member], local)
    own.start()
    for k, peer in enumerate(peers):
        copy_to(k, peer, peer).wait_recv()
    own.wait()
    for copy in sends:
        copy.wait_send()


def per_device(
    cube,
    footprint,
    lift_weight,
    lift_bias,
    spatial_weight,
    spatial_bias,
    spectral_weight,
    head_weight,
):
    micro, planes, pixels = cube.shape
    segments = lax.axis_size("segment")
    tiles = lax.axis_size("tile")
    segment = lax.axis_index("segment")
    tile = lax.axis_index("tile")
    fields = micro // segments
    groups = tiles // fields
    own = planes * fields
    layers = spatial_weight.shape[0] * segments
    reach = layers if groups > 1 else 0
    assert reach <= planes
    wide = own + reach * min(2, groups - 1)
    slots = fields + min(2, groups - 1)

    hbm, vmem = pl.BlockSpec(memory_space=pl.ANY), pl.BlockSpec(memory_space=pltpu.VMEM)
    dma = pltpu.SemaphoreType.DMA
    mine = lax.dynamic_slice_in_dim(cube, segment * fields, fields, 0).astype(BF16)
    parts = (spatial_weight, spatial_bias, spectral_weight)
    x, sw, sb, cw = pl.pallas_call(
        functools.partial(gather, fields, groups),
        out_shape=[jax.ShapeDtypeStruct((slots, planes, pixels), BF16)]
        + [jax.ShapeDtypeStruct((segments,) + part.shape, part.dtype) for part in parts],
        in_specs=[vmem] + [hbm] * 3,
        out_specs=[hbm] * 4,
        scratch_shapes=[
            dma((3, fields)),
            dma((slots,)),
            dma((3, segments)),
            dma((3, segments)),
            dma((4,)),
        ],
        compiler_params=pltpu.CompilerParams(collective_id=0, has_side_effects=True),
    )(mine, *parts)

    first = (tile // fields) * own
    begin = jnp.clip(first - reach, 0, tiles * planes - wide)
    skip = begin - slot_base(tile // fields, fields, slots, tiles) * planes
    origin = jnp.stack([first - begin, skip, segment * fields + tile % fields]).astype(jnp.int32)
    lanes = jnp.tile(jnp.stack([lift_weight, lift_bias, head_weight]), (1, 8))
    scores = run_network(
        own,
        reach,
        wide,
        origin,
        x,
        footprint,
        lanes,
        sw.reshape((layers,) + sw.shape[2:]),
        sb,
        cw.reshape((layers,) + cw.shape[2:]),
    )
    mixed = pl.pallas_call(
        functools.partial(scatter, fields),
        out_shape=jax.ShapeDtypeStruct((fields, planes, pixels), BF16),
        in_specs=[vmem],
        out_specs=vmem,
        scratch_shapes=[dma((fields,)), dma((fields,)), dma(())],
        compiler_params=pltpu.CompilerParams(collective_id=1, has_side_effects=True),
    )(scores)
    return mixed.astype(F32)


def solution(mesh):
    placed = (
        P(None, "tile", None),
        P(),
        P(),
        P(),
        P("segment", None, None),
        P("segment", None),
        P("segment", None, None),
        P(),
    )
    return jax.shard_map(
        per_device,
        mesh=mesh,
        in_specs=placed,
        out_specs=P("segment", "tile", None),
        check_vma=False,
    )
```
